32 devices in a mesh: lat: 4 (over y, x), lon: 8 (over z, core).
Axes of the slice: x: 2, y: 2, z: 4, core: 2. Of those that a mesh axis runs over, the one named last changes fastest.
Arguments:
- thickness: float32 [8, 128, 1024], P(None, 'lat', 'lon'), may hold values from 0.5 to 1.5
- winds: float32 [2, 8, 128, 1024], P(None, None, 'lat', 'lon'), may hold values from -2.5 to 2.5
- tracer_mass: float32 [8, 8, 128, 1024], P(None, None, 'lat', 'lon'), may hold values from -6 to 6
Outputs:
- thickness_out: float32 [8, 128, 1024], P(None, 'lat', 'lon')
- winds_out: float32 [2, 8, 128, 1024], P(None, None, 'lat', 'lon')
- tracer_out: float32 [8, 8, 128, 1024], P(None, None, 'lat', 'lon')
The draws below stay inside these ranges and needn't reach their ends.
All inputs are finite; a program needn't handle non-finite values.
Results may differ from the reference program's by a relative error of at most 0.0003.
Values sent between devices are 32-bit elements; how exact they have to be, the bound alone decides.
A program may use at most 64 MiB of HBM per device.

```python
import math
import jax
import jax.numpy as jnp
from jax import lax

LEV = 8
NTR = 8
SUBSTEPS = 2
NLAT = 128
NLON = 1024


def shard_levels(rng, dims, shards, least, high):
    def one(axis_at, shards_of):
        heights = jax.random.uniform(jax.random.fold_in(jax.random.fold_in(rng, 6), axis_at), (shards_of,), jnp.float32, least / len(shards), high / len(shards))
        return jnp.repeat(jnp.exp(heights), dims[axis_at] // shards_of).reshape((-1,) + (1,) * (len(dims) - axis_at - 1))

    factor_of = one(*shards[0])
    for cut in shards[1:]:
        factor_of = factor_of * one(*cut)
    return factor_of


def noise(stream_key, extent, spread, reach, split=(), held_as=jnp.bfloat16):
    drawn = jax.random.normal(stream_key, extent, jnp.float32) * spread
    if len(split) > 0:
        drawn = shard_levels(stream_key, extent, split, -0.22, 0.18) * drawn
    return jnp.clip(drawn, min=-reach, max=reach).astype(held_as)


def setup_inputs(seed: int = 0) -> dict:
    key_of = jax.random.split(jax.random.key(seed), 4)
    return {
        "thickness": jnp.clip(0.5 + 1.0 * jax.random.uniform(key_of[0], (LEV, NLAT, NLON), jnp.float32) ** shard_levels(key_of[0], (LEV, NLAT, NLON), ((1, 4), (2, 8)), -0.2, 0.2), 0.5, 1.5),
        "winds": noise(key_of[1], (2, LEV, NLAT, NLON), 0.5, 2.5, ((2, 4), (3, 8)), jnp.float32),
        "tracer_mass": noise(key_of[2], (NTR, LEV, NLAT, NLON), 1.0, 6.0, ((2, 4), (3, 8)), jnp.float32),
    }


COUR = 0.25
GRAV = 1.0
FCOR = 1.0


def geopot(thick):
    return GRAV * jnp.flip(jnp.cumsum(jnp.flip(thick, 0), 0), 0)


def upwind(face_speed, behind, centre, forward, beyond):
    return face_speed * jnp.where(face_speed >= 0.0, 5.0 * centre + 2.0 * forward - behind, 5.0 * forward + 2.0 * centre - beyond) / 6.0


def advance(padded, potential, row_start, spacing):
    height = padded.shape[-2]
    columns = padded.shape[-1]
    row_index = (jnp.arange(height) + row_start).astype(jnp.float32)
    center_lat = (row_index[2:height - 2] + 0.5) * spacing - 0.5 * math.pi
    face_lat = (row_index[1:height - 2] + 1.0) * spacing - 0.5 * math.pi
    center_cos = jnp.cos(center_lat)[:, None]
    face_cos = jnp.abs(jnp.cos(face_lat))[:, None]
    coriolis = FCOR * jnp.sin(center_lat)[:, None] * jnp.where(center_cos >= 0.0, 1.0, -1.0)
    band_rows = padded[..., 2:height - 2, :]
    zonal_wind = band_rows[1]
    face_speed = COUR * 0.5 * (zonal_wind[..., 1:columns - 2] + zonal_wind[..., 2:columns - 1])
    zonal_flux = upwind(face_speed, band_rows[..., 0:columns - 3], band_rows[..., 1:columns - 2], band_rows[..., 2:columns - 1], band_rows[..., 3:columns])
    zonal_div = zonal_flux[..., 1:] - zonal_flux[..., :-1]
    column_strip = padded[..., 2:columns - 2]
    merid_wind = column_strip[2]
    merid_speed = COUR * 0.5 * (merid_wind[..., 1:height - 2, :] + merid_wind[..., 2:height - 1, :]) * face_cos
    merid_flux = upwind(merid_speed, column_strip[..., 0:height - 3, :], column_strip[..., 1:height - 2, :], column_strip[..., 2:height - 1, :], column_strip[..., 3:height, :])
    merid_div = (merid_flux[..., 1:, :] - merid_flux[..., :-1, :]) / jnp.abs(center_cos)
    center = padded[..., 2:height - 2, 2:columns - 2]
    advected = center - zonal_div - merid_div
    push_x = COUR * 0.5 * (potential[..., 2:height - 2, 3:columns - 1] - potential[..., 2:height - 2, 1:columns - 3])
    push_y = COUR * 0.5 * (potential[..., 3:height - 1, 2:columns - 2] - potential[..., 1:height - 3, 2:columns - 2])
    east_wind = advected[1] - push_x + COUR * coriolis * center[2]
    north_wind = advected[2] - push_y - COUR * coriolis * center[1]
    return jnp.concatenate([advected[0:1], east_wind[None], north_wind[None], advected[3:]], 0)


def global_pad(field, sign_vector, margin):
    half = field.shape[-1] // 2
    south_rows = jnp.roll(jnp.flip(field[..., 0:margin, :], -2), -half, -1) * sign_vector
    north_rows = jnp.roll(jnp.flip(field[..., field.shape[-2] - margin:, :], -2), -half, -1) * sign_vector
    tall = jnp.concatenate([south_rows, field, north_rows], -2)
    return jnp.concatenate([tall[..., -margin:], tall, tall[..., :margin]], -1)


def reference(thickness, winds, tracer_mass):
    fields = jnp.concatenate([thickness[None], winds, tracer_mass], 0)
    count = fields.shape[0]
    spacing = math.pi / fields.shape[2]
    sign_vector = jnp.where(jnp.arange(count) == 2, -1.0, 1.0).astype(jnp.float32)[:, None, None]
    for substep in range(SUBSTEPS):
        potential = geopot(fields[0])

        def one_level(level):
            layer = lax.dynamic_index_in_dim(fields, level, 1, keepdims=False)
            level_pot = lax.dynamic_index_in_dim(potential, level, 0, keepdims=False)
            return advance(global_pad(layer, sign_vector, 2), global_pad(level_pot, jnp.float32(1.0), 2), -2, spacing)

        fields = jnp.moveaxis(lax.map(one_level, jnp.arange(LEV, dtype=jnp.int32)), 0, 1)
    return fields[0], fields[1:3], fields[3:]
```

```python
import functools
import math

import jax
import jax.numpy as jnp
from jax import lax
from jax.experimental import pallas as pl
from jax.experimental.pallas import tpu as pltpu
from jax.sharding import PartitionSpec as P

SUBSTEPS = 2
COUR = 0.25
GRAV = 1.0
FCOR = 1.0
TG = 2
MESH = pl.DeviceIdType.MESH


def kernel(nlat, nlon, h_hbm, w_hbm, t_hbm, ho, wo, to, hin, win, tin, S, Gs, As, Bs, DXs, DYs, invc, corr, facec,
           rs, rr, cs, cr, hv, wv, tv, in_sem, out_sem, send_sem, recv_sem):
    lev, rows, cols = hin.shape
    ntr = tin.shape[0]
    ngroups = 1 + ntr // TG
    G8 = rows // 8
    stride = rows + 8
    width = 4
    band = lax.axis_index("lat")
    lon = lax.axis_index("lon")
    first = (nlat - band) // nlat
    last = (band + 1) // nlat
    half = nlon // 2
    south = (band - 1 + first, lax.rem(lon + first * half, nlon))
    north = (band + 1 - last, lax.rem(lon + last * half, nlon))
    east = (band, lax.rem(lon + 1, nlon))
    west = (band, lax.rem(lon + nlon - 1, nlon))
    sgn_s = (1 - 2 * first).astype(jnp.float32)
    sgn_n = (1 - 2 * last).astype(jnp.float32)

    barrier = pltpu.get_barrier_semaphore()
    for peer in (south, north, east, west):
        pl.semaphore_signal(barrier, inc=1, device_id=peer, device_id_type=MESH)
    loads = [
        pltpu.make_async_copy(h_hbm, hin, in_sem.at[0]),
        pltpu.make_async_copy(w_hbm, win, in_sem.at[1]),
        pltpu.make_async_copy(t_hbm, tin, in_sem.at[2]),
    ]
    for load in loads:
        load.start()

    spacing = math.pi / (rows * nlat)
    row = lax.broadcasted_iota(jnp.int32, (rows, cols), 0)
    rowf = (row + band * rows).astype(jnp.float32)
    centre_lat = (rowf + 0.5) * spacing - 0.5 * math.pi
    invc[...] = 1.0 / jnp.cos(centre_lat)
    corr[...] = (COUR * FCOR) * jnp.sin(centre_lat)
    face_lat = (rowf + 1.0) * spacing - 0.5 * math.pi
    facec[...] = jnp.abs(jnp.cos(face_lat)) * (COUR * 0.5 / 6.0)
    low_row = (lax.broadcasted_iota(jnp.int32, (8, cols), 0) * 0 + band * rows).astype(jnp.float32)
    fcL = jnp.abs(jnp.cos(low_row * spacing - 0.5 * math.pi)) * (COUR * 0.5 / 6.0)

    lane = lax.broadcasted_iota(jnp.int32, (rows, cols), 1)
    lane8 = lax.broadcasted_iota(jnp.int32, (8, cols), 1)
    slot8 = lane8 // width
    low8 = lax.rem(lane8, width) < 2
    first_lane = lane < 1
    two_lanes = lane < 2
    last_lane = lane >= cols - 1

    def face(speed, behind, centre, forward, beyond):
        return speed * jnp.where(
            speed >= 0.0, 5.0 * centre + 2.0 * forward - behind, 5.0 * forward + 2.0 * centre - beyond
        )

    def pack(acc, x, l):
        for rg in range(G8):
            k = l * G8 + rg
            acc = jnp.where(slot8 == k, pltpu.roll(x[8 * rg : 8 * rg + 8], width * k + 2, 1), acc)
        return acc

    def unpack(packed, l):
        return jnp.concatenate(
            [pltpu.roll(packed, cols - 2 - width * (l * G8 + rg), 1) for rg in range(G8)], 0
        )

    def pack_rows(s, f):
        for r in range(2):
            lo = S[s, f, pl.ds(8 + r + first * (1 - 2 * r), lev, stride=stride), :]
            hi = S[s, f, pl.ds(8 + rows - 2 + r + last * (1 - 2 * r), lev, stride=stride), :]
            if isinstance(f, int) and f == 2:
                lo, hi = lo * sgn_s, hi * sgn_n
            rs[s, 0, f, r] = lo
            rs[s, 1, f, r] = hi

    def copies(s, f0, nf, g):
        fs = pl.ds(f0, nf)

        def one(src, dst, n, m, peer):
            return pltpu.make_async_remote_copy(
                src_ref=src, dst_ref=dst, send_sem=send_sem.at[s, n, g], recv_sem=recv_sem.at[s, m, g],
                device_id=peer, device_id_type=MESH,
            )

        return [
            one(rs.at[s, 0, fs], rr.at[s, 1 - first, fs], 0, 1 - first, south),
            one(rs.at[s, 1, fs], rr.at[s, last, fs], 1, last, north),
            one(cs.at[s, fs], cr.at[s, 0, fs], 2, 2, east),
            one(cs.at[s, fs], cr.at[s, 1, fs], 3, 3, west),
        ]

    def send(s, f0, nf, g):
        for c in copies(s, f0, nf, g):
            c.start()

    def await_halo(s, f0, nf, g):
        fs = pl.ds(f0, nf)
        for m in range(4):
            dst = rr.at[s, m, fs] if m < 2 else cr.at[s, m - 2, fs]
            src = rs.at[s, m, fs] if m < 2 else cs.at[s, fs]
            pltpu.make_async_remote_copy(
                src_ref=src, dst_ref=dst, send_sem=send_sem.at[s, m, g], recv_sem=recv_sem.at[s, m, g],
                device_id=east, device_id_type=MESH,
            ).wait_recv()

    def stage(f, read):
        def level(l, acc):
            x = read(l)
            S[0, f, pl.ds(stride * l + 8, rows), :] = x
            return pack(acc, x, l)

        cs[0, f] = lax.fori_loop(0, lev, level, jnp.zeros((8, cols), jnp.float32), unroll=True)
        pack_rows(0, f)

    loads[0].wait()
    loads[1].wait()
    stage(0, lambda l: hin[l])
    stage(1, lambda l: win[0, l])
    stage(2, lambda l: win[1, l])
    pl.semaphore_wait(barrier, 4)
    send(0, 0, 3, 0)
    loads[2].wait()

    def stage_group(g, c):
        for t in range(TG):
            i = g * TG + t
            stage(3 + i, lambda l: tin[i, l])
        send(0, 3 + g * TG, TG, g + 1)
        return c

    lax.fori_loop(0, ngroups - 1, stage_group, 0)

    for s in range(SUBSTEPS):
        final = s == SUBSTEPS - 1

        def place_rows(f):
            S[s, f, pl.ds(7, lev, stride=stride), :] = rr[s, 0, f, 1]
            S[s, f, pl.ds(8 + rows, lev, stride=stride), :] = rr[s, 1, f, 0]
            S[s, f, pl.ds(9 + rows, lev, stride=stride), :] = rr[s, 1, f, 1]

        def side(f):
            return jnp.where(low8, cr[s, 0, f], cr[s, 1, f]), jnp.where(low8, cr[s, 0, f], cs[s, f])

        def core(f, d=0):
            return lambda l: S[s, f, pl.ds(stride * l + 8 + d, rows), :]

        await_halo(s, 0, 3, 0)
        for f in range(3):
            place_rows(f)
        Cu, Lu = side(1)
        aL = (COUR * 0.5 / 6.0) * (Lu + pltpu.roll(Lu, cols - 1, 1))
        bL = fcL * (rr[s, 0, 2, 1] + S[s, 2, pl.ds(8, lev, stride=stride), :])

        def speeds(l, c):
            u = core(1)(l)
            up = pltpu.roll(jnp.where(first_lane, unpack(Cu, l), u), cols - 1, 1)
            As[l] = (COUR * 0.5 / 6.0) * (u + up)
            Bs[l] = facec[...] * (core(2)(l) + core(2, 1)(l))
            return c

        lax.fori_loop(0, lev, speeds, 0, unroll=True)

        def field(f, write, kind):
            C, L = side(f)
            Lp = pltpu.roll(L, cols - 1, 1)
            FL = face(aL, pltpu.roll(L, 1, 1), L, Lp, pltpu.roll(L, cols - 2, 1))
            x0 = S[s, f, pl.ds(8, lev, stride=stride), :]
            x1 = S[s, f, pl.ds(9, lev, stride=stride), :]
            Gs[pl.ds(7, lev, stride=stride), :] = face(bL, rr[s, 0, f, 0], rr[s, 0, f, 1], x0, x1)

            def level(i, carry):
                l = lev - 1 - i
                acc, dx, dy = carry
                x = core(f)(l)
                H = unpack(C, l)
                xp = pltpu.roll(jnp.where(first_lane, H, x), cols - 1, 1)
                xpp = pltpu.roll(jnp.where(two_lanes, H, x), cols - 2, 1)
                xm = pltpu.roll(jnp.where(last_lane, H, x), 1, 1)
                F = face(As[l], xm, x, xp, xpp)
                Fl = pltpu.roll(jnp.where(last_lane, unpack(FL, l), F), 1, 1)
                ym, yp, ypp = core(f, -1)(l), core(f, 1)(l), core(f, 2)(l)
                G = face(Bs[l], ym, x, yp, ypp)
                Gs[pl.ds(stride * l + 8, rows), :] = G
                Gl = Gs[pl.ds(stride * l + 7, rows), :]
                new = x - (F - Fl) - (G - Gl) * invc[...]
                if kind == 0:
                    dx = dx + (xp - xm)
                    dy = dy + (yp - ym)
                    DXs[l] = dx
                    DYs[l] = dy
                elif kind == 1:
                    new = new - (COUR * 0.5 * GRAV) * DXs[l] + corr[...] * core(2)(l)
                elif kind == 2:
                    new = new - (COUR * 0.5 * GRAV) * DYs[l] - corr[...] * core(1)(l)
                if final:
                    write(l, new)
                else:
                    S[s + 1, f, pl.ds(stride * l + 8, rows), :] = new
                    acc = pack(acc, new, l)
                return acc, dx, dy

            if kind == 0:
                zero = jnp.zeros((rows, cols), jnp.float32)
            else:
                zero = 0
            acc0 = 0 if final else jnp.zeros((8, cols), jnp.float32)
            acc = lax.fori_loop(0, lev, level, (acc0, zero, zero), unroll=True)[0]
            if not final:
                cs[s + 1, f] = acc
                pack_rows(s + 1, f)

        def write_h(l, x):
            hv[l] = x

        def write_u(l, x):
            wv[0, l] = x

        def write_v(l, x):
            wv[1, l] = x

        field(0, write_h, 0)
        field(1, write_u, 1)
        field(2, write_v, 2)
        if final:
            pltpu.make_async_copy(hv, ho, out_sem.at[0]).start()
            pltpu.make_async_copy(wv, wo, out_sem.at[1]).start()
        else:
            send(s + 1, 0, 3, 0)

        def tracers(g, c):
            await_halo(s, 3 + g * TG, TG, g + 1)
            for t in range(TG):
                i = g * TG + t

                def write_t(l, x):
                    tv[i, l] = x

                place_rows(3 + i)
                field(3 + i, write_t, 3)
            if final:
                ts = pl.ds(g * TG, TG)
                pltpu.make_async_copy(tv.at[ts], to.at[ts], out_sem.at[g + 2]).start()
            else:
                send(s + 1, 3 + g * TG, TG, g + 1)
            return c

        lax.fori_loop(0, ngroups - 1, tracers, 0)

    for s in range(SUBSTEPS):
        for c in copies(s, 0, 3, 0):
            c.wait_send()

        def drain(g, c):
            for d in copies(s, 3 + g * TG, TG, g + 1):
                d.wait_send()
            return c

        lax.fori_loop(0, ngroups - 1, drain, 0)
    pltpu.make_async_copy(hv, ho, out_sem.at[0]).wait()
    pltpu.make_async_copy(wv, wo, out_sem.at[1]).wait()

    def flush(g, c):
        ts = pl.ds(g * TG, TG)
        pltpu.make_async_copy(tv.at[ts], to.at[ts], out_sem.at[g + 2]).wait()
        return c

    lax.fori_loop(0, ngroups - 1, flush, 0)


def shards(nlat, nlon, thickness, winds, tracer_mass):
    lev, rows, cols = thickness.shape
    ntr = tracer_mass.shape[0]
    nf = 3 + ntr
    groups = 1 + ntr // TG
    f32 = jnp.float32
    flat = lev * (rows + 8) + 8
    vm = pltpu.VMEM
    return pl.pallas_call(
        functools.partial(kernel, nlat, nlon),
        out_shape=[jax.ShapeDtypeStruct(a.shape, f32) for a in (thickness, winds, tracer_mass)],
        in_specs=[pl.BlockSpec(memory_space=pl.ANY)] * 3,
        out_specs=[pl.BlockSpec(memory_space=pl.ANY)] * 3,
        scratch_shapes=[
            vm(thickness.shape, f32),
            vm(winds.shape, f32),
            vm(tracer_mass.shape, f32),
            vm((SUBSTEPS, nf, flat, cols), f32),
            vm((flat, cols), f32),
            vm((lev, rows, cols), f32),
            vm((lev, rows, cols), f32),
            vm((lev, rows, cols), f32),
            vm((lev, rows, cols), f32),
            vm((rows, cols), f32),
            vm((rows, cols), f32),
            vm((rows, cols), f32),
            vm((SUBSTEPS, 2, nf, 2, lev, cols), f32),
            vm((SUBSTEPS, 2, nf, 2, lev, cols), f32),
            vm((SUBSTEPS, nf, 8, cols), f32),
            vm((SUBSTEPS, 2, nf, 8, cols), f32),
            vm(thickness.shape, f32),
            vm(winds.shape, f32),
            vm(tracer_mass.shape, f32),
            pltpu.SemaphoreType.DMA((3,)),
            pltpu.SemaphoreType.DMA((groups + 1,)),
            pltpu.SemaphoreType.DMA((SUBSTEPS, 4, groups)),
            pltpu.SemaphoreType.DMA((SUBSTEPS, 4, groups)),
        ],
        compiler_params=pltpu.CompilerParams(
            collective_id=0, has_side_effects=True, vmem_limit_bytes=32 * 1024 * 1024
        ),
        cost_estimate=pl.CostEstimate(flops=30_000_000, bytes_accessed=3_000_000, transcendentals=0),
    )(thickness, winds, tracer_mass)


def solution(mesh):
    specs = (P(None, "lat", "lon"), P(None, None, "lat", "lon"), P(None, None, "lat", "lon"))
    return jax.shard_map(
        functools.partial(shards, mesh.shape["lat"], mesh.shape["lon"]),
        mesh=mesh,
        in_specs=specs,
        out_specs=specs,
        check_vma=False,
    )
```

```python
import functools
import math

import jax
import jax.numpy as jnp
from jax import lax
from jax.experimental import pallas as pl
from jax.experimental.pallas import tpu as pltpu
from jax.sharding import PartitionSpec as P

SUBSTEPS = 2
COUR = 0.25
GRAV = 1.0
FCOR = 1.0
TG = 2
MESH = pl.DeviceIdType.MESH


def kernel(nlat, nlon, h_hbm, w_hbm, t_hbm, ho, wo, to, xin, S, Gs, As, Bs, frc, invc, corr, facec,
           rs, rr, cs, cr, out, in_sem, out_sem, send_sem, recv_sem):
    nf, lev, rows, cols = xin.shape
    ngroups = 1 + (nf - 3) // TG
    G8 = rows // 8
    stride = rows + 8
    width = 4
    band = lax.axis_index("lat")
    lon = lax.axis_index("lon")
    first = (nlat - band) // nlat
    last = (band + 1) // nlat
    half = nlon // 2
    south = (band - 1 + first, lax.rem(lon + first * half, nlon))
    north = (band + 1 - last, lax.rem(lon + last * half, nlon))
    east = (band, lax.rem(lon + 1, nlon))
    west = (band, lax.rem(lon + nlon - 1, nlon))

    barrier = pltpu.get_barrier_semaphore()
    for peer in (south, north, east, west):
        pl.semaphore_signal(barrier, inc=1, device_id=peer, device_id_type=MESH)
    loads = [
        pltpu.make_async_copy(h_hbm, xin.at[0], in_sem.at[0]),
        pltpu.make_async_copy(w_hbm, xin.at[pl.ds(1, 2)], in_sem.at[1]),
        pltpu.make_async_copy(t_hbm, xin.at[pl.ds(3, nf - 3)], in_sem.at[2]),
    ]
    for load in loads:
        load.start()

    spacing = math.pi / (rows * nlat)
    row = lax.broadcasted_iota(jnp.int32, (rows, cols), 0)
    rowf = (row + band * rows).astype(jnp.float32)
    centre_lat = (rowf + 0.5) * spacing - 0.5 * math.pi
    invc[...] = 1.0 / jnp.cos(centre_lat)
    corr[...] = (COUR * FCOR) * jnp.sin(centre_lat)
    face_lat = (rowf + 1.0) * spacing - 0.5 * math.pi
    facec[...] = jnp.abs(jnp.cos(face_lat)) * (COUR * 0.5 / 6.0)
    low_row = (lax.broadcasted_iota(jnp.int32, (8, cols), 0) * 0 + band * rows).astype(jnp.float32)
    fcL = jnp.abs(jnp.cos(low_row * spacing - 0.5 * math.pi)) * (COUR * 0.5 / 6.0)
    frc[0] = jnp.zeros((lev, rows, cols), jnp.float32)

    lane = lax.broadcasted_iota(jnp.int32, (rows, cols), 1)
    lane8 = lax.broadcasted_iota(jnp.int32, (8, cols), 1)
    slot8 = lane8 // width
    low8 = lax.rem(lane8, width) < 2
    first_lane = lane < 1
    two_lanes = lane < 2
    last_lane = lane >= cols - 1

    def face(speed, behind, centre, forward, beyond):
        return speed * jnp.where(
            speed >= 0.0, 5.0 * centre + 2.0 * forward - behind, 5.0 * forward + 2.0 * centre - beyond
        )

    def pack(acc, x, l):
        for rg in range(G8):
            k = l * G8 + rg
            acc = jnp.where(slot8 == k, pltpu.roll(x[8 * rg : 8 * rg + 8], width * k + 2, 1), acc)
        return acc

    def unpack(packed, l):
        return jnp.concatenate(
            [pltpu.roll(packed, cols - 2 - width * (l * G8 + rg), 1) for rg in range(G8)], 0
        )

    def wind(f):
        return f * ((nf + 2 - f) // nf)

    def pack_rows(s, f):
        is_v = wind(f) // 2
        for r in range(2):
            lo = S[s, f, pl.ds(8 + r + first * (1 - 2 * r), lev, stride=stride), :]
            hi = S[s, f, pl.ds(8 + rows - 2 + r + last * (1 - 2 * r), lev, stride=stride), :]
            rs[s, 0, f, r] = lo * (1 - 2 * first * is_v).astype(jnp.float32)
            rs[s, 1, f, r] = hi * (1 - 2 * last * is_v).astype(jnp.float32)

    def copies(s, f0, n, g):
        fs = pl.ds(f0, n)

        def one(src, dst, k, m, peer):
            return pltpu.make_async_remote_copy(
                src_ref=src, dst_ref=dst, send_sem=send_sem.at[s, k, g], recv_sem=recv_sem.at[s, m, g],
                device_id=peer, device_id_type=MESH,
            )

        return [
            one(rs.at[s, 0, fs], rr.at[s, 1 - first, fs], 0, 1 - first, south),
            one(rs.at[s, 1, fs], rr.at[s, last, fs], 1, last, north),
            one(cs.at[s, fs], cr.at[s, 0, fs], 2, 2, east),
            one(cs.at[s, fs], cr.at[s, 1, fs], 3, 3, west),
        ]

    def send(s, f0, n, g):
        for c in copies(s, f0, n, g):
            c.start()

    def await_halo(s, f0, n, g):
        fs = pl.ds(f0, n)
        for m in range(4):
            dst = rr.at[s, m, fs] if m < 2 else cr.at[s, m - 2, fs]
            src = rs.at[s, m, fs] if m < 2 else cs.at[s, fs]
            pltpu.make_async_remote_copy(
                src_ref=src, dst_ref=dst, send_sem=send_sem.at[s, m, g], recv_sem=recv_sem.at[s, m, g],
                device_id=east, device_id_type=MESH,
            ).wait_recv()

    def stage(f, c):
        def level(l, acc):
            x = xin[f, l]
            S[0, f, pl.ds(stride * l + 8, rows), :] = x
            return pack(acc, x, l)

        cs[0, f] = lax.fori_loop(0, lev, level, jnp.zeros((8, cols), jnp.float32), unroll=True)
        pack_rows(0, f)
        return c

    loads[0].wait()
    loads[1].wait()
    lax.fori_loop(0, 3, stage, 0)
    pl.semaphore_wait(barrier, 4)
    send(0, 0, 3, 0)
    loads[2].wait()

    def stage_group(g, c):
        lax.fori_loop(3 + g * TG, 3 + (g + 1) * TG, stage, 0)
        send(0, 3 + g * TG, TG, g + 1)
        return c

    lax.fori_loop(0, ngroups - 1, stage_group, 0)

    for s in range(SUBSTEPS):
        final = s == SUBSTEPS - 1

        def place_rows(f):
            S[s, f, pl.ds(7, lev, stride=stride), :] = rr[s, 0, f, 1]
            S[s, f, pl.ds(8 + rows, lev, stride=stride), :] = rr[s, 1, f, 0]
            S[s, f, pl.ds(9 + rows, lev, stride=stride), :] = rr[s, 1, f, 1]

        def side(f):
            return jnp.where(low8, cr[s, 0, f], cr[s, 1, f]), jnp.where(low8, cr[s, 0, f], cs[s, f])

        def core(f, l, d=0):
            return S[s, f, pl.ds(stride * l + 8 + d, rows), :]

        await_halo(s, 0, 3, 0)
        for f in range(3):
            place_rows(f)
        Ch, _ = side(0)
        Cu, Lu = side(1)
        aL = (COUR * 0.5 / 6.0) * (Lu + pltpu.roll(Lu, cols - 1, 1))
        bL = fcL * (rr[s, 0, 2, 1] + S[s, 2, pl.ds(8, lev, stride=stride), :])

        def prepare(i, carry):
            l = lev - 1 - i
            dx, dy = carry
            h, u, v = core(0, l), core(1, l), core(2, l)
            H = unpack(Ch, l)
            hp = pltpu.roll(jnp.where(first_lane, H, h), cols - 1, 1)
            hm = pltpu.roll(jnp.where(last_lane, H, h), 1, 1)
            up = pltpu.roll(jnp.where(first_lane, unpack(Cu, l), u), cols - 1, 1)
            As[l] = (COUR * 0.5 / 6.0) * (u + up)
            Bs[l] = facec[...] * (v + core(2, l, 1))
            dx = dx + (hp - hm)
            dy = dy + (core(0, l, 1) - core(0, l, -1))
            frc[1, l] = corr[...] * v - (COUR * 0.5 * GRAV) * dx
            frc[2, l] = -corr[...] * u - (COUR * 0.5 * GRAV) * dy
            return dx, dy

        zero = jnp.zeros((rows, cols), jnp.float32)
        lax.fori_loop(0, lev, prepare, (zero, zero), unroll=True)

        def field(f, c):
            @pl.when((f >= 3) & (lax.rem(f - 3, TG) == 0))
            def _():
                await_halo(s, f, TG, (f - 3) // TG + 1)

            place_rows(f)
            C, L = side(f)
            Lp = pltpu.roll(L, cols - 1, 1)
            FL = face(aL, pltpu.roll(L, 1, 1), L, Lp, pltpu.roll(L, cols - 2, 1))
            x0 = S[s, f, pl.ds(8, lev, stride=stride), :]
            x1 = S[s, f, pl.ds(9, lev, stride=stride), :]
            Gs[pl.ds(7, lev, stride=stride), :] = face(bL, rr[s, 0, f, 0], rr[s, 0, f, 1], x0, x1)
            kind = wind(f)

            def level(l, acc):
                x = core(f, l)
                H = unpack(C, l)
                xp = pltpu.roll(jnp.where(first_lane, H, x), cols - 1, 1)
                xpp = pltpu.roll(jnp.where(two_lanes, H, x), cols - 2, 1)
                xm = pltpu.roll(jnp.where(last_lane, H, x), 1, 1)
                F = face(As[l], xm, x, xp, xpp)
                Fl = pltpu.roll(jnp.where(last_lane, unpack(FL, l), F), 1, 1)
                G = face(Bs[l], core(f, l, -1), x, core(f, l, 1), core(f, l, 2))
                Gs[pl.ds(stride * l + 8, rows), :] = G
                Gl = Gs[pl.ds(stride * l + 7, rows), :]
                new = x - (F - Fl) - (G - Gl) * invc[...] + frc[kind, l]
                if final:
                    out[f, l] = new
                    return acc
                S[s + 1, f, pl.ds(stride * l + 8, rows), :] = new
                return pack(acc, new, l)

            acc0 = 0 if final else jnp.zeros((8, cols), jnp.float32)
            acc = lax.fori_loop(0, lev, level, acc0, unroll=True)
            if not final:
                cs[s + 1, f] = acc
                pack_rows(s + 1, f)

            @pl.when(f == 2)
            def _():
                if final:
                    pltpu.make_async_copy(out.at[0], ho, out_sem.at[0]).start()
                    pltpu.make_async_copy(out.at[pl.ds(1, 2)], wo, out_sem.at[1]).start()
                else:
                    send(s + 1, 0, 3, 0)

            @pl.when((f >= 3) & (lax.rem(f - 3, TG) == TG - 1))
            def _():
                f0 = f - TG + 1
                g = (f0 - 3) // TG + 1
                if final:
                    pltpu.make_async_copy(
                        out.at[pl.ds(f0, TG)], to.at[pl.ds(f0 - 3, TG)], out_sem.at[g + 1]
                    ).start()
                else:
                    send(s + 1, f0, TG, g)

            return c

        lax.fori_loop(0, nf, field, 0)

    for s in range(SUBSTEPS):
        for c in copies(s, 0, 3, 0):
            c.wait_send()

        def drain(g, c):
            for d in copies(s, 3 + g * TG, TG, g + 1):
                d.wait_send()
            return c

        lax.fori_loop(0, ngroups - 1, drain, 0)
    pltpu.make_async_copy(out.at[0], ho, out_sem.at[0]).wait()
    pltpu.make_async_copy(out.at[pl.ds(1, 2)], wo, out_sem.at[1]).wait()

    def flush(g, c):
        pltpu.make_async_copy(
            out.at[pl.ds(3 + g * TG, TG)], to.at[pl.ds(g * TG, TG)], out_sem.at[g + 2]
        ).wait()
        return c

    lax.fori_loop(0, ngroups - 1, flush, 0)


def shards(nlat, nlon, thickness, winds, tracer_mass):
    lev, rows, cols = thickness.shape
    ntr = tracer_mass.shape[0]
    nf = 3 + ntr
    groups = 1 + ntr // TG
    f32 = jnp.float32
    flat = lev * (rows + 8) + 8
    vm = pltpu.VMEM
    return pl.pallas_call(
        functools.partial(kernel, nlat, nlon),
        out_shape=[jax.ShapeDtypeStruct(a.shape, f32) for a in (thickness, winds, tracer_mass)],
        in_specs=[pl.BlockSpec(memory_space=pl.ANY)] * 3,
        out_specs=[pl.BlockSpec(memory_space=pl.ANY)] * 3,
        scratch_shapes=[
            vm((nf, lev, rows, cols), f32),
            vm((SUBSTEPS, nf, flat, cols), f32),
            vm((flat, cols), f32),
            vm((lev, rows, cols), f32),
            vm((lev, rows, cols), f32),
            vm((3, lev, rows, cols), f32),
            vm((rows, cols), f32),
            vm((rows, cols), f32),
            vm((rows, cols), f32),
            vm((SUBSTEPS, 2, nf, 2, lev, cols), f32),
            vm((SUBSTEPS, 2, nf, 2, lev, cols), f32),
            vm((SUBSTEPS, nf, 8, cols), f32),
            vm((SUBSTEPS, 2, nf, 8, cols), f32),
            vm((nf, lev, rows, cols), f32),
            pltpu.SemaphoreType.DMA((3,)),
            pltpu.SemaphoreType.DMA((groups + 1,)),
            pltpu.SemaphoreType.DMA((SUBSTEPS, 4, groups)),
            pltpu.SemaphoreType.DMA((SUBSTEPS, 4, groups)),
        ],
        compiler_params=pltpu.CompilerParams(
            collective_id=0, has_side_effects=True, vmem_limit_bytes=60 * 1024 * 1024
        ),
        cost_estimate=pl.CostEstimate(flops=30_000_000, bytes_accessed=3_000_000, transcendentals=0),
    )(thickness, winds, tracer_mass)


def solution(mesh):
    specs = (P(None, "lat", "lon"), P(None, None, "lat", "lon"), P(None, None, "lat", "lon"))
    return jax.shard_map(
        functools.partial(shards, mesh.shape["lat"], mesh.shape["lon"]),
        mesh=mesh,
        in_specs=specs,
        out_specs=specs,
        check_vma=False,
    )
```

```python
import functools
import math

import jax
import jax.numpy as jnp
from jax import lax
from jax.experimental import pallas as pl
from jax.experimental.pallas import tpu as pltpu
from jax.sharding import PartitionSpec as P

SUBSTEPS = 2
COUR = 0.25
GRAV = 1.0
FCOR = 1.0
TG = 2
MESH = pl.DeviceIdType.MESH


def kernel(nlat, nlon, h_hbm, w_hbm, t_hbm, out, xin, S, Gs, As, Bs, frc, invc, corr, facec,
           rs, rr, cs, cr, in_sem, send_sem, recv_sem):
    nf, lev, rows, cols = xin.shape
    ngroups = 1 + (nf - 3) // TG
    G8 = rows // 8
    stride = rows + 8
    width = 4
    band = lax.axis_index("lat")
    lon = lax.axis_index("lon")
    first = (nlat - band) // nlat
    last = (band + 1) // nlat
    half = nlon // 2
    south = (band - 1 + first, lax.rem(lon + first * half, nlon))
    north = (band + 1 - last, lax.rem(lon + last * half, nlon))
    east = (band, lax.rem(lon + 1, nlon))
    west = (band, lax.rem(lon + nlon - 1, nlon))

    barrier = pltpu.get_barrier_semaphore()
    for peer in (south, north, east, west):
        pl.semaphore_signal(barrier, inc=1, device_id=peer, device_id_type=MESH)
    loads = [
        pltpu.make_async_copy(h_hbm, xin.at[0], in_sem.at[0]),
        pltpu.make_async_copy(w_hbm, xin.at[pl.ds(1, 2)], in_sem.at[1]),
        pltpu.make_async_copy(t_hbm, xin.at[pl.ds(3, nf - 3)], in_sem.at[2]),
    ]
    for load in loads:
        load.start()

    spacing = math.pi / (rows * nlat)
    row = lax.broadcasted_iota(jnp.int32, (rows, cols), 0)
    rowf = (row + band * rows).astype(jnp.float32)
    centre_lat = (rowf + 0.5) * spacing - 0.5 * math.pi
    invc[...] = 1.0 / jnp.cos(centre_lat)
    corr[...] = (COUR * FCOR) * jnp.sin(centre_lat)
    face_lat = (rowf + 1.0) * spacing - 0.5 * math.pi
    facec[...] = jnp.abs(jnp.cos(face_lat)) * (COUR * 0.5 / 6.0)
    low_row = (lax.broadcasted_iota(jnp.int32, (8, cols), 0) * 0 + band * rows).astype(jnp.float32)
    fcL = jnp.abs(jnp.cos(low_row * spacing - 0.5 * math.pi)) * (COUR * 0.5 / 6.0)
    frc[0] = jnp.zeros((lev, rows, cols), jnp.float32)

    lane = lax.broadcasted_iota(jnp.int32, (rows, cols), 1)
    lane8 = lax.broadcasted_iota(jnp.int32, (8, cols), 1)
    slot8 = lane8 // width
    low8 = lax.rem(lane8, width) < 2
    first_lane = lane < 1
    two_lanes = lane < 2
    last_lane = lane >= cols - 1

    def face(speed, behind, centre, forward, beyond):
        return speed * jnp.where(
            speed >= 0.0, 5.0 * centre + 2.0 * forward - behind, 5.0 * forward + 2.0 * centre - beyond
        )

    def pack(acc, x, l):
        for rg in range(G8):
            k = l * G8 + rg
            acc = jnp.where(slot8 == k, pltpu.roll(x[8 * rg : 8 * rg + 8], width * k + 2, 1), acc)
        return acc

    def unpack(packed, l):
        return jnp.concatenate(
            [pltpu.roll(packed, cols - 2 - width * (l * G8 + rg), 1) for rg in range(G8)], 0
        )

    def wind(f):
        return f * ((nf + 2 - f) // nf)

    def pack_rows(s, f):
        is_v = wind(f) // 2
        for r in range(2):
            lo = S[lax.rem(s, 2), f, pl.ds(8 + r + first * (1 - 2 * r), lev, stride=stride), :]
            hi = S[lax.rem(s, 2), f, pl.ds(8 + rows - 2 + r + last * (1 - 2 * r), lev, stride=stride), :]
            rs[s, 0, f, r] = lo * (1 - 2 * first * is_v).astype(jnp.float32)
            rs[s, 1, f, r] = hi * (1 - 2 * last * is_v).astype(jnp.float32)

    def copies(s, f0, n, g):
        fs = pl.ds(f0, n)

        def one(src, dst, k, m, peer):
            return pltpu.make_async_remote_copy(
                src_ref=src, dst_ref=dst, send_sem=send_sem.at[s, k, g], recv_sem=recv_sem.at[s, m, g],
                device_id=peer, device_id_type=MESH,
            )

        return [
            one(rs.at[s, 0, fs], rr.at[s, 1 - first, fs], 0, 1 - first, south),
            one(rs.at[s, 1, fs], rr.at[s, last, fs], 1, last, north),
            one(cs.at[s, fs], cr.at[s, 0, fs], 2, 2, east),
            one(cs.at[s, fs], cr.at[s, 1, fs], 3, 3, west),
        ]

    def send(s, f0, n, g):
        for c in copies(s, f0, n, g):
            c.start()

    def await_halo(s, f0, n, g):
        fs = pl.ds(f0, n)
        for m in range(4):
            dst = rr.at[s, m, fs] if m < 2 else cr.at[s, m - 2, fs]
            src = rs.at[s, m, fs] if m < 2 else cs.at[s, fs]
            pltpu.make_async_remote_copy(
                src_ref=src, dst_ref=dst, send_sem=send_sem.at[s, m, g], recv_sem=recv_sem.at[s, m, g],
                device_id=east, device_id_type=MESH,
            ).wait_recv()

    def stage(f, c):
        def level(l, acc):
            x = xin[f, l]
            S[0, f, pl.ds(stride * l + 8, rows), :] = x
            return pack(acc, x, l)

        cs[0, f] = lax.fori_loop(0, lev, level, jnp.zeros((8, cols), jnp.float32), unroll=True)
        pack_rows(0, f)
        return c

    loads[0].wait()
    loads[1].wait()
    lax.fori_loop(0, 3, stage, 0)
    pl.semaphore_wait(barrier, 4)
    send(0, 0, 3, 0)
    loads[2].wait()

    def stage_group(g, c):
        lax.fori_loop(3 + g * TG, 3 + (g + 1) * TG, stage, 0)
        send(0, 3 + g * TG, TG, g + 1)
        return c

    lax.fori_loop(0, ngroups - 1, stage_group, 0)

    def substep(s, carry):
        more = s < SUBSTEPS - 1
        spare = 1 - lax.rem(s, 2)

        def place_rows(f):
            S[1 - spare, f, pl.ds(7, lev, stride=stride), :] = rr[s, 0, f, 1]
            S[1 - spare, f, pl.ds(8 + rows, lev, stride=stride), :] = rr[s, 1, f, 0]
            S[1 - spare, f, pl.ds(9 + rows, lev, stride=stride), :] = rr[s, 1, f, 1]

        def side(f):
            return jnp.where(low8, cr[s, 0, f], cr[s, 1, f]), jnp.where(low8, cr[s, 0, f], cs[s, f])

        def core(f, l, d=0):
            return S[1 - spare, f, pl.ds(stride * l + 8 + d, rows), :]

        await_halo(s, 0, 3, 0)
        for f in range(3):
            place_rows(f)
        Ch, _ = side(0)
        Cu, Lu = side(1)
        aL = (COUR * 0.5 / 6.0) * (Lu + pltpu.roll(Lu, cols - 1, 1))
        bL = fcL * (rr[s, 0, 2, 1] + S[1 - spare, 2, pl.ds(8, lev, stride=stride), :])

        def prepare(i, carry):
            l = lev - 1 - i
            dx, dy = carry
            h, u, v = core(0, l), core(1, l), core(2, l)
            H = unpack(Ch, l)
            hp = pltpu.roll(jnp.where(first_lane, H, h), cols - 1, 1)
            hm = pltpu.roll(jnp.where(last_lane, H, h), 1, 1)
            up = pltpu.roll(jnp.where(first_lane, unpack(Cu, l), u), cols - 1, 1)
            As[l] = (COUR * 0.5 / 6.0) * (u + up)
            Bs[l] = facec[...] * (v + core(2, l, 1))
            dx = dx + (hp - hm)
            dy = dy + (core(0, l, 1) - core(0, l, -1))
            frc[1, l] = corr[...] * v - (COUR * 0.5 * GRAV) * dx
            frc[2, l] = -corr[...] * u - (COUR * 0.5 * GRAV) * dy
            return dx, dy

        zero = jnp.zeros((rows, cols), jnp.float32)
        lax.fori_loop(0, lev, prepare, (zero, zero), unroll=True)

        def field(f, c):
            @pl.when((f >= 3) & (lax.rem(f - 3, TG) == 0))
            def _():
                await_halo(s, f, TG, (f - 3) // TG + 1)

            place_rows(f)
            C, L = side(f)
            Lp = pltpu.roll(L, cols - 1, 1)
            FL = face(aL, pltpu.roll(L, 1, 1), L, Lp, pltpu.roll(L, cols - 2, 1))
            x0 = S[1 - spare, f, pl.ds(8, lev, stride=stride), :]
            x1 = S[1 - spare, f, pl.ds(9, lev, stride=stride), :]
            Gs[pl.ds(7, lev, stride=stride), :] = face(bL, rr[s, 0, f, 0], rr[s, 0, f, 1], x0, x1)
            kind = wind(f)

            def level(l, acc):
                x = core(f, l)
                H = unpack(C, l)
                xp = pltpu.roll(jnp.where(first_lane, H, x), cols - 1, 1)
                xpp = pltpu.roll(jnp.where(two_lanes, H, x), cols - 2, 1)
                xm = pltpu.roll(jnp.where(last_lane, H, x), 1, 1)
                F = face(As[l], xm, x, xp, xpp)
                Fl = pltpu.roll(jnp.where(last_lane, unpack(FL, l), F), 1, 1)
                G = face(Bs[l], core(f, l, -1), x, core(f, l, 1), core(f, l, 2))
                Gs[pl.ds(stride * l + 8, rows), :] = G
                Gl = Gs[pl.ds(stride * l + 7, rows), :]
                new = x - (F - Fl) - (G - Gl) * invc[...] + frc[kind, l]
                out[f, l] = new
                S[spare, f, pl.ds(stride * l + 8, rows), :] = new
                return pack(acc, new, l)

            acc = lax.fori_loop(0, lev, level, jnp.zeros((8, cols), jnp.float32), unroll=True)

            @pl.when(more)
            def _():
                cs[s + 1, f] = acc
                pack_rows(s + 1, f)

            @pl.when(more & (f == 2))
            def _():
                send(s + 1, 0, 3, 0)

            @pl.when(more & (f >= 3) & (lax.rem(f - 3, TG) == TG - 1))
            def _():
                send(s + 1, f - TG + 1, TG, (f - 3) // TG + 1)

            return c

        lax.fori_loop(0, nf, field, 0)
        return carry

    lax.fori_loop(0, SUBSTEPS, substep, 0)

    for s in range(SUBSTEPS):
        for c in copies(s, 0, 3, 0):
            c.wait_send()

        def drain(g, c):
            for d in copies(s, 3 + g * TG, TG, g + 1):
                d.wait_send()
            return c

        lax.fori_loop(0, ngroups - 1, drain, 0)

def store_kernel(state, ho, wo, to, sem):
    moves = [
        pltpu.make_async_copy(state.at[pl.ds(3, to.shape[0])], to, sem.at[0]),
        pltpu.make_async_copy(state.at[pl.ds(1, 2)], wo, sem.at[1]),
        pltpu.make_async_copy(state.at[0], ho, sem.at[2]),
    ]
    for move in moves:
        move.start()
    for move in moves:
        move.wait()


def shards(nlat, nlon, thickness, winds, tracer_mass):
    lev, rows, cols = thickness.shape
    ntr = tracer_mass.shape[0]
    nf = 3 + ntr
    groups = 1 + ntr // TG
    f32 = jnp.float32
    flat = lev * (rows + 8) + 8
    vm = pltpu.VMEM
    state = pl.pallas_call(
        functools.partial(kernel, nlat, nlon),
        out_shape=pltpu.VMEM((nf, lev, rows, cols), f32),
        in_specs=[pl.BlockSpec(memory_space=pltpu.HBM)] * 3,
        out_specs=pl.BlockSpec(memory_space=pltpu.VMEM),
        scratch_shapes=[
            vm((nf, lev, rows, cols), f32),
            vm((SUBSTEPS, nf, flat, cols), f32),
            vm((flat, cols), f32),
            vm((lev, rows, cols), f32),
            vm((lev, rows, cols), f32),
            vm((3, lev, rows, cols), f32),
            vm((rows, cols), f32),
            vm((rows, cols), f32),
            vm((rows, cols), f32),
            vm((SUBSTEPS, 2, nf, 2, lev, cols), f32),
            vm((SUBSTEPS, 2, nf, 2, lev, cols), f32),
            vm((SUBSTEPS, nf, 8, cols), f32),
            vm((SUBSTEPS, 2, nf, 8, cols), f32),
            pltpu.SemaphoreType.DMA((3,)),
            pltpu.SemaphoreType.DMA((SUBSTEPS, 4, groups)),
            pltpu.SemaphoreType.DMA((SUBSTEPS, 4, groups)),
        ],
        compiler_params=pltpu.CompilerParams(
            collective_id=0, has_side_effects=True, vmem_limit_bytes=56 * 1024 * 1024
        ),
        cost_estimate=pl.CostEstimate(flops=30_000_000, bytes_accessed=3_000_000, transcendentals=0),
    )(thickness, winds, tracer_mass)
    return pl.pallas_call(
        store_kernel,
        out_shape=[jax.ShapeDtypeStruct(a.shape, f32) for a in (thickness, winds, tracer_mass)],
        in_specs=[pl.BlockSpec(memory_space=pltpu.VMEM)],
        out_specs=[pl.BlockSpec(memory_space=pltpu.HBM)] * 3,
        scratch_shapes=[pltpu.SemaphoreType.DMA((3,))],
        compiler_params=pltpu.CompilerParams(vmem_limit_bytes=8 * 1024 * 1024),
    )(state)


def solution(mesh):
    specs = (P(None, "lat", "lon"), P(None, None, "lat", "lon"), P(None, None, "lat", "lon"))
    return jax.shard_map(
        functools.partial(shards, mesh.shape["lat"], mesh.shape["lon"]),
        mesh=mesh,
        in_specs=specs,
        out_specs=specs,
        check_vma=False,
    )
```

```python
import functools
import math

import jax
import jax.numpy as jnp
from jax import lax
from jax.experimental import pallas as pl
from jax.experimental.pallas import tpu as pltpu
from jax.sharding import PartitionSpec as P

SUBSTEPS = 2
COUR = 0.25
GRAV = 1.0
FCOR = 1.0
TG = 2
MESH = pl.DeviceIdType.MESH


def kernel(nlat, nlon, h_hbm, w_hbm, t_hbm, out, xin, S0, S1, Gs, As, Bs, frc, invc, corr, facec,
           rs, rr, cs, cr, in_sem, send_sem, recv_sem):
    nf, lev, rows, cols = xin.shape
    S = (S0, S1)
    ngroups = 1 + (nf - 3) // TG
    G8 = rows // 8
    stride = rows + 8
    width = 4
    band = lax.axis_index("lat")
    lon = lax.axis_index("lon")
    first = (nlat - band) // nlat
    last = (band + 1) // nlat
    half = nlon // 2
    south = (band - 1 + first, lax.rem(lon + first * half, nlon))
    north = (band + 1 - last, lax.rem(lon + last * half, nlon))
    east = (band, lax.rem(lon + 1, nlon))
    west = (band, lax.rem(lon + nlon - 1, nlon))

    barrier = pltpu.get_barrier_semaphore()
    for peer in (south, north, east, west):
        pl.semaphore_signal(barrier, inc=1, device_id=peer, device_id_type=MESH)
    loads = [
        pltpu.make_async_copy(h_hbm, xin.at[0], in_sem.at[0]),
        pltpu.make_async_copy(w_hbm, xin.at[pl.ds(1, 2)], in_sem.at[1]),
        pltpu.make_async_copy(t_hbm, xin.at[pl.ds(3, nf - 3)], in_sem.at[2]),
    ]
    for load in loads:
        load.start()

    spacing = math.pi / (rows * nlat)
    row = lax.broadcasted_iota(jnp.int32, (rows, cols), 0)
    rowf = (row + band * rows).astype(jnp.float32)
    centre_lat = (rowf + 0.5) * spacing - 0.5 * math.pi
    invc[...] = 1.0 / jnp.cos(centre_lat)
    corr[...] = (COUR * FCOR) * jnp.sin(centre_lat)
    face_lat = (rowf + 1.0) * spacing - 0.5 * math.pi
    facec[...] = jnp.abs(jnp.cos(face_lat)) * (COUR * 0.5 / 6.0)
    low_row = (lax.broadcasted_iota(jnp.int32, (8, cols), 0) * 0 + band * rows).astype(jnp.float32)
    fcL = jnp.abs(jnp.cos(low_row * spacing - 0.5 * math.pi)) * (COUR * 0.5 / 6.0)
    frc[0] = jnp.zeros((lev, rows, cols), jnp.float32)

    lane = lax.broadcasted_iota(jnp.int32, (rows, cols), 1)
    lane8 = lax.broadcasted_iota(jnp.int32, (8, cols), 1)
    slot8 = lane8 // width
    low8 = lax.rem(lane8, width) < 2
    first_lane = lane < 1
    two_lanes = lane < 2
    last_lane = lane >= cols - 1

    def face(speed, behind, centre, forward, beyond):
        return speed * jnp.where(
            speed >= 0.0, 5.0 * centre + 2.0 * forward - behind, 5.0 * forward + 2.0 * centre - beyond
        )

    def pack(acc, x, l):
        for rg in range(G8):
            k = l * G8 + rg
            acc = jnp.where(slot8 == k, pltpu.roll(x[8 * rg : 8 * rg + 8], width * k + 2, 1), acc)
        return acc

    def unpack(packed, l):
        return jnp.concatenate(
            [pltpu.roll(packed, cols - 2 - width * (l * G8 + rg), 1) for rg in range(G8)], 0
        )

    def wind(f):
        return f * ((nf + 2 - f) // nf)

    def pack_rows(s, f):
        is_v = wind(f) // 2
        for r in range(2):
            lo = S[s][f, pl.ds(8 + r + first * (1 - 2 * r), lev, stride=stride), :]
            hi = S[s][f, pl.ds(8 + rows - 2 + r + last * (1 - 2 * r), lev, stride=stride), :]
            rs[s, 0, f, r] = lo * (1 - 2 * first * is_v).astype(jnp.float32)
            rs[s, 1, f, r] = hi * (1 - 2 * last * is_v).astype(jnp.float32)

    def copies(s, f0, n, g):
        fs = pl.ds(f0, n)

        def one(src, dst, k, m, peer):
            return pltpu.make_async_remote_copy(
                src_ref=src, dst_ref=dst, send_sem=send_sem.at[s, k, g], recv_sem=recv_sem.at[s, m, g],
                device_id=peer, device_id_type=MESH,
            )

        return [
            one(rs.at[s, 0, fs], rr.at[s, 1 - first, fs], 0, 1 - first, south),
            one(rs.at[s, 1, fs], rr.at[s, last, fs], 1, last, north),
            one(cs.at[s, fs], cr.at[s, 0, fs], 2, 2, east),
            one(cs.at[s, fs], cr.at[s, 1, fs], 3, 3, west),
        ]

    def send(s, f0, n, g):
        for c in copies(s, f0, n, g):
            c.start()

    def await_halo(s, f0, n, g):
        fs = pl.ds(f0, n)
        for m in range(4):
            dst = rr.at[s, m, fs] if m < 2 else cr.at[s, m - 2, fs]
            src = rs.at[s, m, fs] if m < 2 else cs.at[s, fs]
            pltpu.make_async_remote_copy(
                src_ref=src, dst_ref=dst, send_sem=send_sem.at[s, m, g], recv_sem=recv_sem.at[s, m, g],
                device_id=east, device_id_type=MESH,
            ).wait_recv()

    def stage(f, c):
        def level(l, acc):
            x = xin[f, l]
            S[0][f, pl.ds(stride * l + 8, rows), :] = x
            return pack(acc, x, l)

        cs[0, f] = lax.fori_loop(0, lev, level, jnp.zeros((8, cols), jnp.float32), unroll=True)
        pack_rows(0, f)
        return c

    loads[0].wait()
    loads[1].wait()
    lax.fori_loop(0, 3, stage, 0)
    pl.semaphore_wait(barrier, 4)
    send(0, 0, 3, 0)
    loads[2].wait()

    def stage_group(g, c):
        lax.fori_loop(3 + g * TG, 3 + (g + 1) * TG, stage, 0)
        send(0, 3 + g * TG, TG, g + 1)
        return c

    lax.fori_loop(0, ngroups - 1, stage_group, 0)

    for s in range(SUBSTEPS):
        final = s == SUBSTEPS - 1

        def place_rows(f):
            S[s][f, pl.ds(7, lev, stride=stride), :] = rr[s, 0, f, 1]
            S[s][f, pl.ds(8 + rows, lev, stride=stride), :] = rr[s, 1, f, 0]
            S[s][f, pl.ds(9 + rows, lev, stride=stride), :] = rr[s, 1, f, 1]

        def side(f):
            return jnp.where(low8, cr[s, 0, f], cr[s, 1, f]), jnp.where(low8, cr[s, 0, f], cs[s, f])

        def core(f, l, d=0):
            return S[s][f, pl.ds(stride * l + 8 + d, rows), :]

        await_halo(s, 0, 3, 0)
        for f in range(3):
            place_rows(f)
        Ch, _ = side(0)
        Cu, Lu = side(1)
        aL = (COUR * 0.5 / 6.0) * (Lu + pltpu.roll(Lu, cols - 1, 1))
        bL = fcL * (rr[s, 0, 2, 1] + S[s][2, pl.ds(8, lev, stride=stride), :])

        def prepare(i, carry):
            l = lev - 1 - i
            dx, dy = carry
            h, u, v = core(0, l), core(1, l), core(2, l)
            H = unpack(Ch, l)
            hp = pltpu.roll(jnp.where(first_lane, H, h), cols - 1, 1)
            hm = pltpu.roll(jnp.where(last_lane, H, h), 1, 1)
            up = pltpu.roll(jnp.where(first_lane, unpack(Cu, l), u), cols - 1, 1)
            As[l] = (COUR * 0.5 / 6.0) * (u + up)
            Bs[l] = facec[...] * (v + core(2, l, 1))
            dx = dx + (hp - hm)
            dy = dy + (core(0, l, 1) - core(0, l, -1))
            frc[1, l] = corr[...] * v - (COUR * 0.5 * GRAV) * dx
            frc[2, l] = -corr[...] * u - (COUR * 0.5 * GRAV) * dy
            return dx, dy

        zero = jnp.zeros((rows, cols), jnp.float32)
        lax.fori_loop(0, lev, prepare, (zero, zero), unroll=True)

        def field(f, c):
            @pl.when((f >= 3) & (lax.rem(f - 3, TG) == 0))
            def _():
                await_halo(s, f, TG, (f - 3) // TG + 1)

            place_rows(f)
            C, L = side(f)
            Lp = pltpu.roll(L, cols - 1, 1)
            FL = face(aL, pltpu.roll(L, 1, 1), L, Lp, pltpu.roll(L, cols - 2, 1))
            x0 = S[s][f, pl.ds(8, lev, stride=stride), :]
            x1 = S[s][f, pl.ds(9, lev, stride=stride), :]
            Gs[pl.ds(7, lev, stride=stride), :] = face(bL, rr[s, 0, f, 0], rr[s, 0, f, 1], x0, x1)
            kind = wind(f)

            def level(l, acc):
                x = core(f, l)
                H = unpack(C, l)
                xp = pltpu.roll(jnp.where(first_lane, H, x), cols - 1, 1)
                xpp = pltpu.roll(jnp.where(two_lanes, H, x), cols - 2, 1)
                xm = pltpu.roll(jnp.where(last_lane, H, x), 1, 1)
                F = face(As[l], xm, x, xp, xpp)
                Fl = pltpu.roll(jnp.where(last_lane, unpack(FL, l), F), 1, 1)
                G = face(Bs[l], core(f, l, -1), x, core(f, l, 1), core(f, l, 2))
                Gs[pl.ds(stride * l + 8, rows), :] = G
                Gl = Gs[pl.ds(stride * l + 7, rows), :]
                new = x - (F - Fl) - (G - Gl) * invc[...] + frc[kind, l]
                if final:
                    out[f, l] = new
                    return acc
                S[s + 1][f, pl.ds(stride * l + 8, rows), :] = new
                return pack(acc, new, l)

            acc0 = 0 if final else jnp.zeros((8, cols), jnp.float32)
            acc = lax.fori_loop(0, lev, level, acc0, unroll=True)
            if not final:
                cs[s + 1, f] = acc
                pack_rows(s + 1, f)

            if final:
                return c

            @pl.when(f == 2)
            def _():
                send(s + 1, 0, 3, 0)

            @pl.when((f >= 3) & (lax.rem(f - 3, TG) == TG - 1))
            def _():
                send(s + 1, f - TG + 1, TG, (f - 3) // TG + 1)

            return c

        lax.fori_loop(0, nf, field, 0)

    for s in range(SUBSTEPS):
        for c in copies(s, 0, 3, 0):
            c.wait_send()

        def drain(g, c):
            for d in copies(s, 3 + g * TG, TG, g + 1):
                d.wait_send()
            return c

        lax.fori_loop(0, ngroups - 1, drain, 0)

def store_kernel(state, ho, wo, to, sem):
    moves = [
        pltpu.make_async_copy(state.at[pl.ds(3, to.shape[0])], to, sem.at[0]),
        pltpu.make_async_copy(state.at[pl.ds(1, 2)], wo, sem.at[1]),
        pltpu.make_async_copy(state.at[0], ho, sem.at[2]),
    ]
    for move in moves:
        move.start()
    for move in moves:
        move.wait()


def shards(nlat, nlon, thickness, winds, tracer_mass):
    lev, rows, cols = thickness.shape
    ntr = tracer_mass.shape[0]
    nf = 3 + ntr
    groups = 1 + ntr // TG
    f32 = jnp.float32
    flat = lev * (rows + 8) + 8
    vm = pltpu.VMEM
    state = pl.pallas_call(
        functools.partial(kernel, nlat, nlon),
        out_shape=pltpu.VMEM((nf, lev, rows, cols), f32),
        in_specs=[pl.BlockSpec(memory_space=pltpu.HBM)] * 3,
        out_specs=pl.BlockSpec(memory_space=pltpu.VMEM),
        scratch_shapes=[
            vm((nf, lev, rows, cols), f32),
            vm((nf, flat, cols), f32),
            vm((nf, flat, cols), f32),
            vm((flat, cols), f32),
            vm((lev, rows, cols), f32),
            vm((lev, rows, cols), f32),
            vm((3, lev, rows, cols), f32),
            vm((rows, cols), f32),
            vm((rows, cols), f32),
            vm((rows, cols), f32),
            vm((SUBSTEPS, 2, nf, 2, lev, cols), f32),
            vm((SUBSTEPS, 2, nf, 2, lev, cols), f32),
            vm((SUBSTEPS, nf, 8, cols), f32),
            vm((SUBSTEPS, 2, nf, 8, cols), f32),
            pltpu.SemaphoreType.DMA((3,)),
            pltpu.SemaphoreType.DMA((SUBSTEPS, 4, groups)),
            pltpu.SemaphoreType.DMA((SUBSTEPS, 4, groups)),
        ],
        compiler_params=pltpu.CompilerParams(
            collective_id=0, has_side_effects=True, vmem_limit_bytes=56 * 1024 * 1024
        ),
        cost_estimate=pl.CostEstimate(flops=30_000_000, bytes_accessed=3_000_000, transcendentals=0),
    )(thickness, winds, tracer_mass)
    return pl.pallas_call(
        store_kernel,
        out_shape=[jax.ShapeDtypeStruct(a.shape, f32) for a in (thickness, winds, tracer_mass)],
        in_specs=[pl.BlockSpec(memory_space=pltpu.VMEM)],
        out_specs=[pl.BlockSpec(memory_space=pltpu.HBM)] * 3,
        scratch_shapes=[pltpu.SemaphoreType.DMA((3,))],
        compiler_params=pltpu.CompilerParams(vmem_limit_bytes=8 * 1024 * 1024),
    )(state)


def solution(mesh):
    specs = (P(None, "lat", "lon"), P(None, None, "lat", "lon"), P(None, None, "lat", "lon"))
    return jax.shard_map(
        functools.partial(shards, mesh.shape["lat"], mesh.shape["lon"]),
        mesh=mesh,
        in_specs=specs,
        out_specs=specs,
        check_vma=False,
    )
```

```python
import functools
import math

import jax
import jax.numpy as jnp
from jax import lax
from jax.experimental import pallas as pl
from jax.experimental.pallas import tpu as pltpu
from jax.sharding import PartitionSpec as P

SUBSTEPS = 2
COUR = 0.25
GRAV = 1.0
FCOR = 1.0
TG = 2
MESH = pl.DeviceIdType.MESH


def kernel(nlat, nlon, h_hbm, w_hbm, t_hbm, out, xin, S0, S1, Gs, As, Bs, frc, invc, corr, facec,
           rs, rr, cs, cr, in_sem, send_sem, recv_sem):
    nf, lev, rows, cols = xin.shape
    S = (S0, S1)
    ngroups = 1 + (nf - 3) // TG
    G8 = rows // 8
    stride = rows + 8
    width = 4
    band = lax.axis_index("lat")
    lon = lax.axis_index("lon")
    first = (nlat - band) // nlat
    last = (band + 1) // nlat
    half = nlon // 2
    south = (band - 1 + first, lax.rem(lon + first * half, nlon))
    north = (band + 1 - last, lax.rem(lon + last * half, nlon))
    east = (band, lax.rem(lon + 1, nlon))
    west = (band, lax.rem(lon + nlon - 1, nlon))

    barrier = pltpu.get_barrier_semaphore()
    for peer in (south, north, east, west):
        pl.semaphore_signal(barrier, inc=1, device_id=peer, device_id_type=MESH)
    loads = [
        pltpu.make_async_copy(h_hbm, xin.at[0], in_sem.at[0]),
        pltpu.make_async_copy(w_hbm, xin.at[pl.ds(1, 2)], in_sem.at[1]),
        pltpu.make_async_copy(t_hbm, xin.at[pl.ds(3, nf - 3)], in_sem.at[2]),
    ]
    for load in loads:
        load.start()

    spacing = math.pi / (rows * nlat)
    row = lax.broadcasted_iota(jnp.int32, (rows, cols), 0)
    rowf = (row + band * rows).astype(jnp.float32)
    centre_lat = (rowf + 0.5) * spacing - 0.5 * math.pi
    invc[...] = 1.0 / jnp.cos(centre_lat)
    corr[...] = (COUR * FCOR) * jnp.sin(centre_lat)
    face_lat = (rowf + 1.0) * spacing - 0.5 * math.pi
    facec[...] = jnp.abs(jnp.cos(face_lat)) * (COUR * 0.5 / 6.0)
    low_row = (lax.broadcasted_iota(jnp.int32, (8, cols), 0) * 0 + band * rows).astype(jnp.float32)
    fcL = jnp.abs(jnp.cos(low_row * spacing - 0.5 * math.pi)) * (COUR * 0.5 / 6.0)
    frc[0] = jnp.zeros((lev, rows, cols), jnp.float32)

    lane = lax.broadcasted_iota(jnp.int32, (rows, cols), 1)
    lane8 = lax.broadcasted_iota(jnp.int32, (8, cols), 1)
    slot8 = lane8 // width
    low8 = lax.rem(lane8, width) < 2
    first_lane = lane < 1
    two_lanes = lane < 2
    last_lane = lane >= cols - 1

    def face(speed, behind, centre, forward, beyond):
        along = speed >= 0.0
        near = jnp.where(along, centre, forward)
        far = jnp.where(along, behind, beyond)
        return speed * (2.0 * (centre + forward) + (3.0 * near - far))

    def pack(acc, x, l):
        for rg in range(G8):
            k = l * G8 + rg
            acc = jnp.where(slot8 == k, pltpu.roll(x[8 * rg : 8 * rg + 8], width * k + 2, 1), acc)
        return acc

    def unpack(packed, l):
        return jnp.concatenate(
            [pltpu.roll(packed, cols - 2 - width * (l * G8 + rg), 1) for rg in range(G8)], 0
        )

    def wind(f):
        return f * ((nf + 2 - f) // nf)

    def pack_rows(s, f):
        is_v = wind(f) // 2
        for r in range(2):
            lo = S[s][f, pl.ds(8 + r + first * (1 - 2 * r), lev, stride=stride), :]
            hi = S[s][f, pl.ds(8 + rows - 2 + r + last * (1 - 2 * r), lev, stride=stride), :]
            rs[s, 0, f, r] = lo * (1 - 2 * first * is_v).astype(jnp.float32)
            rs[s, 1, f, r] = hi * (1 - 2 * last * is_v).astype(jnp.float32)

    def copies(s, f0, n, g):
        fs = pl.ds(f0, n)

        def one(src, dst, k, m, peer):
            return pltpu.make_async_remote_copy(
                src_ref=src, dst_ref=dst, send_sem=send_sem.at[s, k, g], recv_sem=recv_sem.at[s, m, g],
                device_id=peer, device_id_type=MESH,
            )

        return [
            one(rs.at[s, 0, fs], rr.at[s, 1 - first, fs], 0, 1 - first, south),
            one(rs.at[s, 1, fs], rr.at[s, last, fs], 1, last, north),
            one(cs.at[s, fs], cr.at[s, 0, fs], 2, 2, east),
            one(cs.at[s, fs], cr.at[s, 1, fs], 3, 3, west),
        ]

    def send(s, f0, n, g):
        for c in copies(s, f0, n, g):
            c.start()

    def await_halo(s, f0, n, g):
        fs = pl.ds(f0, n)
        for m in range(4):
            dst = rr.at[s, m, fs] if m < 2 else cr.at[s, m - 2, fs]
            src = rs.at[s, m, fs] if m < 2 else cs.at[s, fs]
            pltpu.make_async_remote_copy(
                src_ref=src, dst_ref=dst, send_sem=send_sem.at[s, m, g], recv_sem=recv_sem.at[s, m, g],
                device_id=east, device_id_type=MESH,
            ).wait_recv()

    def stage(f, c):
        def level(l, acc):
            x = xin[f, l]
            S[0][f, pl.ds(stride * l + 8, rows), :] = x
            return pack(acc, x, l)

        cs[0, f] = lax.fori_loop(0, lev, level, jnp.zeros((8, cols), jnp.float32), unroll=True)
        pack_rows(0, f)
        return c

    loads[0].wait()
    loads[1].wait()
    lax.fori_loop(0, 3, stage, 0)
    pl.semaphore_wait(barrier, 4)
    send(0, 0, 3, 0)
    loads[2].wait()

    def stage_group(g, c):
        lax.fori_loop(3 + g * TG, 3 + (g + 1) * TG, stage, 0)
        send(0, 3 + g * TG, TG, g + 1)
        return c

    lax.fori_loop(0, ngroups - 1, stage_group, 0)

    for s in range(SUBSTEPS):
        final = s == SUBSTEPS - 1

        def place_rows(f):
            S[s][f, pl.ds(7, lev, stride=stride), :] = rr[s, 0, f, 1]
            S[s][f, pl.ds(8 + rows, lev, stride=stride), :] = rr[s, 1, f, 0]
            S[s][f, pl.ds(9 + rows, lev, stride=stride), :] = rr[s, 1, f, 1]

        def side(f):
            return jnp.where(low8, cr[s, 0, f], cr[s, 1, f]), jnp.where(low8, cr[s, 0, f], cs[s, f])

        def core(f, l, d=0):
            return S[s][f, pl.ds(stride * l + 8 + d, rows), :]

        await_halo(s, 0, 3, 0)
        for f in range(3):
            place_rows(f)
        Ch, _ = side(0)
        Cu, Lu = side(1)
        aL = (COUR * 0.5 / 6.0) * (Lu + pltpu.roll(Lu, cols - 1, 1))
        bL = fcL * (rr[s, 0, 2, 1] + S[s][2, pl.ds(8, lev, stride=stride), :])

        def prepare(i, carry):
            l = lev - 1 - i
            dx, dy = carry
            h, u, v = core(0, l), core(1, l), core(2, l)
            H = unpack(Ch, l)
            hp = pltpu.roll(jnp.where(first_lane, H, h), cols - 1, 1)
            hm = pltpu.roll(jnp.where(last_lane, H, h), 1, 1)
            up = pltpu.roll(jnp.where(first_lane, unpack(Cu, l), u), cols - 1, 1)
            As[l] = (COUR * 0.5 / 6.0) * (u + up)
            Bs[l] = facec[...] * (v + core(2, l, 1))
            dx = dx + (hp - hm)
            dy = dy + (core(0, l, 1) - core(0, l, -1))
            frc[1, l] = corr[...] * v - (COUR * 0.5 * GRAV) * dx
            frc[2, l] = -corr[...] * u - (COUR * 0.5 * GRAV) * dy
            return dx, dy

        zero = jnp.zeros((rows, cols), jnp.float32)
        lax.fori_loop(0, lev, prepare, (zero, zero), unroll=True)

        def field(f, c):
            @pl.when((f >= 3) & (lax.rem(f - 3, TG) == 0))
            def _():
                await_halo(s, f, TG, (f - 3) // TG + 1)

            place_rows(f)
            C, L = side(f)
            Lp = pltpu.roll(L, cols - 1, 1)
            FL = face(aL, pltpu.roll(L, 1, 1), L, Lp, pltpu.roll(L, cols - 2, 1))
            x0 = S[s][f, pl.ds(8, lev, stride=stride), :]
            x1 = S[s][f, pl.ds(9, lev, stride=stride), :]
            Gs[pl.ds(7, lev, stride=stride), :] = face(bL, rr[s, 0, f, 0], rr[s, 0, f, 1], x0, x1)
            kind = wind(f)

            def level(l, acc):
                x = core(f, l)
                H = unpack(C, l)
                xp = pltpu.roll(jnp.where(first_lane, H, x), cols - 1, 1)
                xpp = pltpu.roll(jnp.where(two_lanes, H, x), cols - 2, 1)
                xm = pltpu.roll(jnp.where(last_lane, H, x), 1, 1)
                F = face(As[l], xm, x, xp, xpp)
                Fl = pltpu.roll(jnp.where(last_lane, unpack(FL, l), F), 1, 1)
                G = face(Bs[l], core(f, l, -1), x, core(f, l, 1), core(f, l, 2))
                Gs[pl.ds(stride * l + 8, rows), :] = G
                Gl = Gs[pl.ds(stride * l + 7, rows), :]
                new = x - (F - Fl) - (G - Gl) * invc[...] + frc[kind, l]
                if final:
                    out[f, l] = new
                    return acc
                S[s + 1][f, pl.ds(stride * l + 8, rows), :] = new
                return pack(acc, new, l)

            acc0 = 0 if final else jnp.zeros((8, cols), jnp.float32)
            acc = lax.fori_loop(0, lev, level, acc0, unroll=True)
            if not final:
                cs[s + 1, f] = acc
                pack_rows(s + 1, f)

            if final:
                return c

            @pl.when(f == 2)
            def _():
                send(s + 1, 0, 3, 0)

            @pl.when((f >= 3) & (lax.rem(f - 3, TG) == TG - 1))
            def _():
                send(s + 1, f - TG + 1, TG, (f - 3) // TG + 1)

            return c

        lax.fori_loop(0, nf, field, 0)

    for s in range(SUBSTEPS):
        for c in copies(s, 0, 3, 0):
            c.wait_send()

        def drain(g, c):
            for d in copies(s, 3 + g * TG, TG, g + 1):
                d.wait_send()
            return c

        lax.fori_loop(0, ngroups - 1, drain, 0)

def store_kernel(state, ho, wo, to, sem):
    moves = [
        pltpu.make_async_copy(state.at[pl.ds(3, to.shape[0])], to, sem.at[0]),
        pltpu.make_async_copy(state.at[pl.ds(1, 2)], wo, sem.at[1]),
        pltpu.make_async_copy(state.at[0], ho, sem.at[2]),
    ]
    for move in moves:
        move.start()
    for move in moves:
        move.wait()


def shards(nlat, nlon, thickness, winds, tracer_mass):
    lev, rows, cols = thickness.shape
    ntr = tracer_mass.shape[0]
    nf = 3 + ntr
    groups = 1 + ntr // TG
    f32 = jnp.float32
    flat = lev * (rows + 8) + 8
    vm = pltpu.VMEM
    state = pl.pallas_call(
        functools.partial(kernel, nlat, nlon),
        out_shape=pltpu.VMEM((nf, lev, rows, cols), f32),
        in_specs=[pl.BlockSpec(memory_space=pltpu.HBM)] * 3,
        out_specs=pl.BlockSpec(memory_space=pltpu.VMEM),
        scratch_shapes=[
            vm((nf, lev, rows, cols), f32),
            vm((nf, flat, cols), f32),
            vm((nf, flat, cols), f32),
            vm((flat, cols), f32),
            vm((lev, rows, cols), f32),
            vm((lev, rows, cols), f32),
            vm((3, lev, rows, cols), f32),
            vm((rows, cols), f32),
            vm((rows, cols), f32),
            vm((rows, cols), f32),
            vm((SUBSTEPS, 2, nf, 2, lev, cols), f32),
            vm((SUBSTEPS, 2, nf, 2, lev, cols), f32),
            vm((SUBSTEPS, nf, 8, cols), f32),
            vm((SUBSTEPS, 2, nf, 8, cols), f32),
            pltpu.SemaphoreType.DMA((3,)),
            pltpu.SemaphoreType.DMA((SUBSTEPS, 4, groups)),
            pltpu.SemaphoreType.DMA((SUBSTEPS, 4, groups)),
        ],
        compiler_params=pltpu.CompilerParams(
            collective_id=0, has_side_effects=True, vmem_limit_bytes=56 * 1024 * 1024
        ),
        cost_estimate=pl.CostEstimate(flops=30_000_000, bytes_accessed=3_000_000, transcendentals=0),
    )(thickness, winds, tracer_mass)
    return pl.pallas_call(
        store_kernel,
        out_shape=[jax.ShapeDtypeStruct(a.shape, f32) for a in (thickness, winds, tracer_mass)],
        in_specs=[pl.BlockSpec(memory_space=pltpu.VMEM)],
        out_specs=[pl.BlockSpec(memory_space=pltpu.HBM)] * 3,
        scratch_shapes=[pltpu.SemaphoreType.DMA((3,))],
        compiler_params=pltpu.CompilerParams(vmem_limit_bytes=8 * 1024 * 1024),
    )(state)


def solution(mesh):
    specs = (P(None, "lat", "lon"), P(None, None, "lat", "lon"), P(None, None, "lat", "lon"))
    return jax.shard_map(
        functools.partial(shards, mesh.shape["lat"], mesh.shape["lon"]),
        mesh=mesh,
        in_specs=specs,
        out_specs=specs,
        check_vma=False,
    )
```

```python
import functools
import math

import jax
import jax.numpy as jnp
from jax import lax
from jax.experimental import pallas as pl
from jax.experimental.pallas import tpu as pltpu
from jax.sharding import PartitionSpec as P

SUBSTEPS = 2
COUR = 0.25
GRAV = 1.0
FCOR = 1.0
TG = 1
MESH = pl.DeviceIdType.MESH


def kernel(nlat, nlon, h_hbm, w_hbm, t_hbm, out, xin, S0, S1, Gs, As, Bs, frc, invc, corr, facec,
           rs, rr, cs, cr, in_sem, send_sem, recv_sem):
    nf, lev, rows, cols = xin.shape
    S = (S0, S1)
    ngroups = 1 + (nf - 3) // TG
    G8 = rows // 8
    stride = rows + 8
    width = 4
    band = lax.axis_index("lat")
    lon = lax.axis_index("lon")
    first = (nlat - band) // nlat
    last = (band + 1) // nlat
    half = nlon // 2
    south = (band - 1 + first, lax.rem(lon + first * half, nlon))
    north = (band + 1 - last, lax.rem(lon + last * half, nlon))
    east = (band, lax.rem(lon + 1, nlon))
    west = (band, lax.rem(lon + nlon - 1, nlon))

    barrier = pltpu.get_barrier_semaphore()
    for peer in (south, north, east, west):
        pl.semaphore_signal(barrier, inc=1, device_id=peer, device_id_type=MESH)
    loads = [
        pltpu.make_async_copy(h_hbm, xin.at[0], in_sem.at[0]),
        pltpu.make_async_copy(w_hbm, xin.at[pl.ds(1, 2)], in_sem.at[1]),
        pltpu.make_async_copy(t_hbm, xin.at[pl.ds(3, nf - 3)], in_sem.at[2]),
    ]
    for load in loads:
        load.start()

    spacing = math.pi / (rows * nlat)
    row = lax.broadcasted_iota(jnp.int32, (rows, cols), 0)
    rowf = (row + band * rows).astype(jnp.float32)
    centre_lat = (rowf + 0.5) * spacing - 0.5 * math.pi
    invc[...] = 1.0 / jnp.cos(centre_lat)
    corr[...] = (COUR * FCOR) * jnp.sin(centre_lat)
    face_lat = (rowf + 1.0) * spacing - 0.5 * math.pi
    facec[...] = jnp.abs(jnp.cos(face_lat)) * (COUR * 0.5 / 6.0)
    low_row = (lax.broadcasted_iota(jnp.int32, (8, cols), 0) * 0 + band * rows).astype(jnp.float32)
    fcL = jnp.abs(jnp.cos(low_row * spacing - 0.5 * math.pi)) * (COUR * 0.5 / 6.0)
    frc[0] = jnp.zeros((lev, rows, cols), jnp.float32)

    lane = lax.broadcasted_iota(jnp.int32, (rows, cols), 1)
    lane8 = lax.broadcasted_iota(jnp.int32, (8, cols), 1)
    slot8 = lane8 // width
    low8 = lax.rem(lane8, width) < 2
    first_lane = lane < 1
    two_lanes = lane < 2
    last_lane = lane >= cols - 1

    def face(speed, behind, centre, forward, beyond):
        along = speed >= 0.0
        near = jnp.where(along, centre, forward)
        far = jnp.where(along, behind, beyond)
        return speed * (2.0 * (centre + forward) + (3.0 * near - far))

    def pack(acc, x, l):
        for rg in range(G8):
            k = l * G8 + rg
            acc = jnp.where(slot8 == k, pltpu.roll(x[8 * rg : 8 * rg + 8], width * k + 2, 1), acc)
        return acc

    def unpack(packed, l):
        return jnp.concatenate(
            [pltpu.roll(packed, cols - 2 - width * (l * G8 + rg), 1) for rg in range(G8)], 0
        )

    def wind(f):
        return f * ((nf + 2 - f) // nf)

    def pack_rows(s, f):
        is_v = wind(f) // 2
        for r in range(2):
            lo = S[s][f, pl.ds(8 + r + first * (1 - 2 * r), lev, stride=stride), :]
            hi = S[s][f, pl.ds(8 + rows - 2 + r + last * (1 - 2 * r), lev, stride=stride), :]
            rs[s, 0, f, r] = lo * (1 - 2 * first * is_v).astype(jnp.float32)
            rs[s, 1, f, r] = hi * (1 - 2 * last * is_v).astype(jnp.float32)

    def copies(s, f0, n, g):
        fs = pl.ds(f0, n)

        def one(src, dst, k, m, peer):
            return pltpu.make_async_remote_copy(
                src_ref=src, dst_ref=dst, send_sem=send_sem.at[s, k, g], recv_sem=recv_sem.at[s, m, g],
                device_id=peer, device_id_type=MESH,
            )

        return [
            one(rs.at[s, 0, fs], rr.at[s, 1 - first, fs], 0, 1 - first, south),
            one(rs.at[s, 1, fs], rr.at[s, last, fs], 1, last, north),
            one(cs.at[s, fs], cr.at[s, 0, fs], 2, 2, east),
            one(cs.at[s, fs], cr.at[s, 1, fs], 3, 3, west),
        ]

    def send(s, f0, n, g):
        for c in copies(s, f0, n, g):
            c.start()

    def await_halo(s, f0, n, g):
        fs = pl.ds(f0, n)
        for m in range(4):
            dst = rr.at[s, m, fs] if m < 2 else cr.at[s, m - 2, fs]
            src = rs.at[s, m, fs] if m < 2 else cs.at[s, fs]
            pltpu.make_async_remote_copy(
                src_ref=src, dst_ref=dst, send_sem=send_sem.at[s, m, g], recv_sem=recv_sem.at[s, m, g],
                device_id=east, device_id_type=MESH,
            ).wait_recv()

    def stage(f, c):
        def level(l, acc):
            x = xin[f, l]
            S[0][f, pl.ds(stride * l + 8, rows), :] = x
            return pack(acc, x, l)

        cs[0, f] = lax.fori_loop(0, lev, level, jnp.zeros((8, cols), jnp.float32), unroll=True)
        pack_rows(0, f)
        return c

    loads[0].wait()
    loads[1].wait()
    lax.fori_loop(0, 3, stage, 0)
    pl.semaphore_wait(barrier, 4)
    send(0, 0, 3, 0)
    loads[2].wait()

    def stage_group(g, c):
        lax.fori_loop(3 + g * TG, 3 + (g + 1) * TG, stage, 0)
        send(0, 3 + g * TG, TG, g + 1)
        return c

    lax.fori_loop(0, ngroups - 1, stage_group, 0)

    for s in range(SUBSTEPS):
        final = s == SUBSTEPS - 1

        def place_rows(f):
            S[s][f, pl.ds(7, lev, stride=stride), :] = rr[s, 0, f, 1]
            S[s][f, pl.ds(8 + rows, lev, stride=stride), :] = rr[s, 1, f, 0]
            S[s][f, pl.ds(9 + rows, lev, stride=stride), :] = rr[s, 1, f, 1]

        def side(f):
            return jnp.where(low8, cr[s, 0, f], cr[s, 1, f]), jnp.where(low8, cr[s, 0, f], cs[s, f])

        def core(f, l, d=0):
            return S[s][f, pl.ds(stride * l + 8 + d, rows), :]

        await_halo(s, 0, 3, 0)
        for f in range(3):
            place_rows(f)
        Ch, _ = side(0)
        Cu, Lu = side(1)
        aL = (COUR * 0.5 / 6.0) * (Lu + pltpu.roll(Lu, cols - 1, 1))
        bL = fcL * (rr[s, 0, 2, 1] + S[s][2, pl.ds(8, lev, stride=stride), :])

        def prepare(i, carry):
            l = lev - 1 - i
            dx, dy = carry
            h, u, v = core(0, l), core(1, l), core(2, l)
            H = unpack(Ch, l)
            hp = pltpu.roll(jnp.where(first_lane, H, h), cols - 1, 1)
            hm = pltpu.roll(jnp.where(last_lane, H, h), 1, 1)
            up = pltpu.roll(jnp.where(first_lane, unpack(Cu, l), u), cols - 1, 1)
            As[l] = (COUR * 0.5 / 6.0) * (u + up)
            Bs[l] = facec[...] * (v + core(2, l, 1))
            dx = dx + (hp - hm)
            dy = dy + (core(0, l, 1) - core(0, l, -1))
            frc[1, l] = corr[...] * v - (COUR * 0.5 * GRAV) * dx
            frc[2, l] = -corr[...] * u - (COUR * 0.5 * GRAV) * dy
            return dx, dy

        zero = jnp.zeros((rows, cols), jnp.float32)
        lax.fori_loop(0, lev, prepare, (zero, zero), unroll=True)

        def field(f, c):
            @pl.when((f >= 3) & (lax.rem(f - 3, TG) == 0))
            def _():
                await_halo(s, f, TG, (f - 3) // TG + 1)

            place_rows(f)
            C, L = side(f)
            Lp = pltpu.roll(L, cols - 1, 1)
            FL = face(aL, pltpu.roll(L, 1, 1), L, Lp, pltpu.roll(L, cols - 2, 1))
            x0 = S[s][f, pl.ds(8, lev, stride=stride), :]
            x1 = S[s][f, pl.ds(9, lev, stride=stride), :]
            Gs[pl.ds(7, lev, stride=stride), :] = face(bL, rr[s, 0, f, 0], rr[s, 0, f, 1], x0, x1)
            kind = wind(f)

            def level(l, acc):
                x = core(f, l)
                H = unpack(C, l)
                xp = pltpu.roll(jnp.where(first_lane, H, x), cols - 1, 1)
                xpp = pltpu.roll(jnp.where(two_lanes, H, x), cols - 2, 1)
                xm = pltpu.roll(jnp.where(last_lane, H, x), 1, 1)
                F = face(As[l], xm, x, xp, xpp)
                Fl = pltpu.roll(jnp.where(last_lane, unpack(FL, l), F), 1, 1)
                G = face(Bs[l], core(f, l, -1), x, core(f, l, 1), core(f, l, 2))
                Gs[pl.ds(stride * l + 8, rows), :] = G
                Gl = Gs[pl.ds(stride * l + 7, rows), :]
                new = x - (F - Fl) - (G - Gl) * invc[...] + frc[kind, l]
                if final:
                    out[f, l] = new
                    return acc
                S[s + 1][f, pl.ds(stride * l + 8, rows), :] = new
                return pack(acc, new, l)

            acc0 = 0 if final else jnp.zeros((8, cols), jnp.float32)
            acc = lax.fori_loop(0, lev, level, acc0, unroll=True)
            if not final:
                cs[s + 1, f] = acc
                pack_rows(s + 1, f)

            if final:
                return c

            @pl.when(f == 2)
            def _():
                send(s + 1, 0, 3, 0)

            @pl.when((f >= 3) & (lax.rem(f - 3, TG) == TG - 1))
            def _():
                send(s + 1, f - TG + 1, TG, (f - 3) // TG + 1)

            return c

        lax.fori_loop(0, nf, field, 0)

    for s in range(SUBSTEPS):
        for c in copies(s, 0, 3, 0):
            c.wait_send()

        def drain(g, c):
            for d in copies(s, 3 + g * TG, TG, g + 1):
                d.wait_send()
            return c

        lax.fori_loop(0, ngroups - 1, drain, 0)

def store_kernel(state, ho, wo, to, sem):
    moves = [
        pltpu.make_async_copy(state.at[pl.ds(3, to.shape[0])], to, sem.at[0]),
        pltpu.make_async_copy(state.at[pl.ds(1, 2)], wo, sem.at[1]),
        pltpu.make_async_copy(state.at[0], ho, sem.at[2]),
    ]
    for move in moves:
        move.start()
    for move in moves:
        move.wait()


def shards(nlat, nlon, thickness, winds, tracer_mass):
    lev, rows, cols = thickness.shape
    ntr = tracer_mass.shape[0]
    nf = 3 + ntr
    groups = 1 + ntr // TG
    f32 = jnp.float32
    flat = lev * (rows + 8) + 8
    vm = pltpu.VMEM
    state = pl.pallas_call(
        functools.partial(kernel, nlat, nlon),
        out_shape=pltpu.VMEM((nf, lev, rows, cols), f32),
        in_specs=[pl.BlockSpec(memory_space=pltpu.HBM)] * 3,
        out_specs=pl.BlockSpec(memory_space=pltpu.VMEM),
        scratch_shapes=[
            vm((nf, lev, rows, cols), f32),
            vm((nf, flat, cols), f32),
            vm((nf, flat, cols), f32),
            vm((flat, cols), f32),
            vm((lev, rows, cols), f32),
            vm((lev, rows, cols), f32),
            vm((3, lev, rows, cols), f32),
            vm((rows, cols), f32),
            vm((rows, cols), f32),
            vm((rows, cols), f32),
            vm((SUBSTEPS, 2, nf, 2, lev, cols), f32),
            vm((SUBSTEPS, 2, nf, 2, lev, cols), f32),
            vm((SUBSTEPS, nf, 8, cols), f32),
            vm((SUBSTEPS, 2, nf, 8, cols), f32),
            pltpu.SemaphoreType.DMA((3,)),
            pltpu.SemaphoreType.DMA((SUBSTEPS, 4, groups)),
            pltpu.SemaphoreType.DMA((SUBSTEPS, 4, groups)),
        ],
        compiler_params=pltpu.CompilerParams(
            collective_id=0, has_side_effects=True, vmem_limit_bytes=56 * 1024 * 1024
        ),
        cost_estimate=pl.CostEstimate(flops=30_000_000, bytes_accessed=3_000_000, transcendentals=0),
    )(thickness, winds, tracer_mass)
    return pl.pallas_call(
        store_kernel,
        out_shape=[jax.ShapeDtypeStruct(a.shape, f32) for a in (thickness, winds, tracer_mass)],
        in_specs=[pl.BlockSpec(memory_space=pltpu.VMEM)],
        out_specs=[pl.BlockSpec(memory_space=pltpu.HBM)] * 3,
        scratch_shapes=[pltpu.SemaphoreType.DMA((3,))],
        compiler_params=pltpu.CompilerParams(vmem_limit_bytes=8 * 1024 * 1024),
    )(state)


def solution(mesh):
    specs = (P(None, "lat", "lon"), P(None, None, "lat", "lon"), P(None, None, "lat", "lon"))
    return jax.shard_map(
        functools.partial(shards, mesh.shape["lat"], mesh.shape["lon"]),
        mesh=mesh,
        in_specs=specs,
        out_specs=specs,
        check_vma=False,
    )
```
